32 devices in a mesh: lon: 8 (over z, x), lat: 4 (over y, core).
Axes of the slice: x: 2, y: 2, z: 4, core: 2. Of those that a mesh axis runs over, the one named last changes fastest.
Arguments:
- fields: float32 [5, 4, 128, 1024], P(None, None, 'lat', 'lon'), may hold values from -6 to 6
- depth: int32 [128], P('lat'), may hold values from 0 to 96, as said below
- frac: float32 [4, 128, 1024], P(None, 'lat', 'lon'), may hold values from 0 to 1
- helm: float32 [4, 128, 1024], P(None, 'lat', 'lon'), may hold values from 0.1 to 2
Outputs:
- departed: float32 [5, 4, 128, 1024], P(None, None, 'lat', 'lon')
- pressure: float32 [4, 128, 1024], P(None, 'lat', 'lon')
The draws below stay inside these ranges and needn't reach their ends.
Inputs may be any that keep to these rules, and one draw needn't show every extreme that they name: All rows of an aligned band of 8 latitude rows share one depth. A band's depth is either 96 (a jet band) or at most 32, and may be 0. Among the 32 rows of one device (aligned blocks) at most 1 band is a jet band, and in every draw some block has exactly 1.
All inputs are finite; a program needn't handle non-finite values.
Results may differ from the reference program's by a relative error of at most 0.0003.
Values sent between devices are 32-bit elements; how exact they have to be, the bound alone decides.
A program may use at most 128 MiB of HBM per device.

```python
import math
import jax
import jax.numpy as jnp

CLAT = 32
LEV = 4
BAND = 8
MAXD = 96
SHALLOW = 32
JETS = 1
NLON = 1024
NLAT = 128


def draw_depth(key, part):
    nbands = NLAT // BAND
    per_block = CLAT // BAND
    blocks = NLAT // CLAT
    key_base, key_count, key_order, key_top = jax.random.split(key, 4)
    base = jax.random.randint(key_base, (nbands,), 0, SHALLOW + 1)
    count = jax.random.randint(key_count, (blocks,), 0, JETS + 1)
    top = jax.random.randint(key_top, (), 0, blocks)
    is_top = jnp.arange(blocks) == top
    count = jnp.where(is_top, JETS, jnp.minimum(count, per_block - 1))
    order = jax.vmap(lambda k: jax.random.permutation(k, per_block))(jax.random.split(key_order, blocks))
    jet = (order < count[:, None]).reshape(nbands)
    still = ((order == per_block - 1) & jnp.logical_not(is_top)[:, None]).reshape(nbands)
    bands = jnp.where(jet, MAXD, jnp.where(still, 0, base))
    return jnp.repeat(bands, BAND).astype(jnp.int32)


def block_scale(rng, shape, cuts, low, top_value):
    gain = 1.0
    for axis_at, shards_of in cuts:
        steps = jax.random.uniform(jax.random.fold_in(jax.random.fold_in(rng, 6), axis_at), (shards_of,), jnp.float32, low / len(cuts), top_value / len(cuts))
        gain = gain * jnp.repeat(jnp.exp(steps), shape[axis_at] // shards_of).reshape((-1,) + (1,) * (len(shape) - 1 - axis_at))
    return gain


def bell_draw(own_key, dims, width, limit, cuts=(), held_as=jnp.bfloat16):
    array = jax.random.normal(own_key, dims, jnp.float32) * width
    if len(cuts) > 0:
        array = block_scale(own_key, dims, cuts, -0.22, 0.18) * array
    return jnp.clip(array, min=-limit, max=limit).astype(held_as)


def setup_inputs(seed: int = 0) -> dict:
    splits = jax.random.split(jax.random.key(seed), 5)
    return {
        "fields": bell_draw(splits[0], (5, LEV, NLAT, NLON), 1.0, 6.0, ((2, 4), (3, 8)), jnp.float32),
        "depth": draw_depth(jax.random.fold_in(splits[4], 71), 0),
        "frac": jnp.clip(1.0 * jax.random.uniform(splits[2], (LEV, NLAT, NLON), jnp.float32) ** block_scale(splits[2], (LEV, NLAT, NLON), ((1, 4), (2, 8)), -0.2, 0.2), 0.0, 1.0),
        "helm": jnp.clip(jnp.exp(math.log(2.0) - 2.9957323 * jax.random.uniform(splits[3], (LEV, NLAT, NLON), jnp.float32) ** block_scale(splits[3], (LEV, NLAT, NLON), ((1, 4), (2, 8)), -0.2, 0.2)), 0.1, 2.0),
    }


def interp_weights(frac):
    s = -frac
    return [s * (s + 1.0) * (s + 2.0) / 6.0, -(s - 1.0) * (s + 1.0) * (s + 2.0) / 2.0, (s - 1.0) * s * (s + 2.0) / 2.0, -(s - 1.0) * s * (s + 1.0) / 6.0]


def lat_next(field):
    zero_row = jnp.zeros_like(field[:, :1, :])
    return jnp.concatenate([field[:, 1:, :], zero_row], axis=1)


def lat_prev(field):
    zero_row = jnp.zeros_like(field[:, :1, :])
    return jnp.concatenate([zero_row, field[:, :-1, :]], axis=1)


def reference(fields, depth, frac, helm):
    nlon = fields.shape[3]
    column = jnp.arange(nlon, dtype=jnp.int32)
    weights = interp_weights(frac)
    offsets = [-1, 0, 1, 2]
    results = []
    for which in range(5):
        field = fields[which]
        total = jnp.zeros_like(field)
        for offset, weight in zip(offsets, weights):
            index = jnp.mod(column[None, :] - depth[:, None].astype(jnp.int32) - offset, nlon).astype(jnp.int32)
            index = jnp.broadcast_to(index[None], field.shape)
            total = total + weight * jnp.take_along_axis(field, index, axis=2)
        results.append(total)
    departed = jnp.stack(results)
    u_wind, v_wind, phi = departed[0], departed[1], departed[3]
    div = 0.5 * (jnp.roll(u_wind, -1, axis=2) - jnp.roll(u_wind, 1, axis=2) + lat_next(v_wind) - lat_prev(v_wind))
    rhs = phi - 0.5 * div
    pressure = phi
    for sweep in range(2):
        beside_all = jnp.roll(pressure, -1, axis=2) + jnp.roll(pressure, 1, axis=2) + lat_next(pressure) + lat_prev(pressure)
        pressure = (rhs + beside_all) / (4.0 + helm)
    return departed, pressure
```

```python
import functools

import jax
import jax.numpy as jnp
from jax import lax
from jax.experimental import pallas as pl
from jax.experimental.pallas import tpu as pltpu
from jax.sharding import PartitionSpec as P

BAND = 8
SHALLOW = 32
LANES = 128
NEAR = SHALLOW + 4
F32 = jnp.float32
MESH = pl.DeviceIdType.MESH
HALO_FIELDS = (0, 1, 3)
SPARE = 108


def turn(x, shift):
    shift %= LANES
    return x if shift == 0 else pltpu.roll(x, shift, axis=1)


def lane_of(shape):
    return lax.broadcasted_iota(jnp.int32, shape, len(shape) - 1)


def jet_band(depth_ref, bands):
    jet = jnp.int32(0)
    for b in range(1, bands):
        jet = jnp.where(depth_ref[b * BAND] > SHALLOW, b, jet)
    return jet


def exchange(lev, clat, depth_ref, fields_hbm, frac_hbm, helm_hbm,
             main_o, edge_o, above_o, below_o, la_o, lb_o, ra_o, rb_o,
             fields, frac, helm, main, edge, top, bottom, dtop, dbottom, gtop, gbottom,
             in_sem, send_sem, recv_sem):
    bands = clat // BAND
    loads = [
        pltpu.make_async_copy(src, dst, in_sem.at[i])
        for i, (src, dst) in enumerate(((fields_hbm, fields), (frac_hbm, frac), (helm_hbm, helm)))
    ]
    for load in loads:
        load.start()
    nlon, nlat = lax.axis_size("lon"), lax.axis_size("lat")
    i, j = lax.axis_index("lon"), lax.axis_index("lat")
    east, west = lax.rem(i + 1, nlon), lax.rem(i + nlon - 1, nlon)
    south, north = lax.rem(j + 1, nlat), lax.rem(j + nlat - 1, nlat)
    peers = [{"lon": a, "lat": b} for a, b in (
        (east, j), (west, j), (i, north), (i, south),
        (east, north), (east, south), (west, north), (west, south))]
    barrier = pltpu.get_barrier_semaphore()
    for peer in peers:
        pl.semaphore_signal(barrier, inc=1, device_id=peer, device_id_type=MESH)

    def copy(n, src, dst, peer):
        return pltpu.make_async_remote_copy(
            src_ref=src, dst_ref=dst, send_sem=send_sem.at[n], recv_sem=recv_sem.at[n],
            device_id=peers[peer], device_id_type=MESH)

    copies = [
        copy(0, main, main_o, 0),
        copy(1, edge, edge_o, 1),
        copy(2, top, below_o, 2),
        copy(3, bottom, above_o, 3),
        copy(4, dtop, lb_o, 4),
        copy(5, dbottom, la_o, 5),
        copy(6, gtop, rb_o, 6),
        copy(7, gbottom, ra_o, 7),
    ]
    jet = jet_band(depth_ref, bands)
    for load in loads:
        load.wait()
    nf = 5 * lev * BAND
    lane = lane_of((nf, LANES))
    jet = jnp.full((nf, LANES), jet)
    x = [fields[:, :, pl.ds(b * BAND, BAND), :].reshape(nf, LANES) for b in range(bands)]
    whole = x[0]
    for b in range(1, bands):
        whole = jnp.where(jet == b, x[b], whole)
    main[0] = whole.reshape(5, lev, BAND, LANES)
    packed = None
    for slot in range(bands - 1):
        y = jnp.where(jet > slot, x[slot], x[slot + 1])
        y = turn(y, slot * NEAR + NEAR - LANES)
        packed = y if packed is None else jnp.where(lane >= slot * NEAR, y, packed)
    main[1] = packed.reshape(5, lev, BAND, LANES)
    nk = lev * BAND
    lane = lane_of((nk, LANES))
    rest = main[1, 0].reshape(nk, LANES)
    for b in range(bands):
        at = SPARE + 3 * b
        rows = pl.ds(b * BAND, BAND)
        fr = turn(frac[:, rows, :].reshape(nk, LANES), at - (LANES - 2))
        he = turn(helm[:, rows, :].reshape(nk, LANES), at + 2 - (LANES - 1))
        rest = jnp.where((lane >= at) & (lane < at + 2), fr, rest)
        rest = jnp.where(lane == at + 2, he, rest)
    main[1, 0] = rest.reshape(lev, BAND, LANES)
    pl.semaphore_wait(barrier, len(peers))
    copies[0].start()

    acc = jnp.zeros((nk, LANES), F32)
    for b in range(bands):
        rows = pl.ds(b * BAND, BAND)
        for n in range(7):
            src = fields[n, :, rows, :] if n < 5 else (frac if n == 5 else helm)[:, rows, :]
            at = 32 * b + (17 if n == 6 else 3 * n)
            wide = 3 if n < 5 else 7 - n
            acc = jnp.where((lane >= at) & (lane < at + wide), turn(src.reshape(nk, LANES), at), acc)
    edge[...] = acc.reshape(lev, BAND, LANES)
    copies[1].start()

    lane8 = lane_of((2 * lev, LANES))
    for row, mine, diag, thin, n, at_depth in (
            (0, top, dtop, gtop, 0, 0), (clat - 2, bottom, dbottom, gbottom, 1, clat - 1)):
        for q in range(5):
            src = fields.at[HALO_FIELDS[q]] if q < 3 else (frac if q == 3 else helm)
            for k in range(lev):
                mine[q, 2 * k:2 * k + 2, :] = src[k, row:row + 2, :]
        mine[5] = jnp.full((2 * lev, LANES), depth_ref[at_depth].astype(F32))
        copies[2 + n].start()
        u = jnp.where(lane8 < 2, turn(mine[3], 2), mine[0])
        diag[0] = jnp.where(lane8 == 2, turn(mine[4], 3), u)
        diag[1] = mine[1]
        diag[2] = mine[2]
        copies[4 + n].start()
        g = mine[0]
        for q in range(1, 5):
            at = 11 if q == 4 else 3 * q
            g = jnp.where(lane8 >= at, turn(mine[q], at), g)
        thin[...] = g
        copies[6 + n].start()
    for c in copies:
        c.wait()


def interp_weights(frac):
    s = -frac
    return [
        s * (s + 1.0) * (s + 2.0) / 6.0,
        -(s - 1.0) * (s + 1.0) * (s + 2.0) / 2.0,
        (s - 1.0) * s * (s + 2.0) / 2.0,
        -(s - 1.0) * s * (s + 1.0) / 6.0,
    ]


def depart(own, left, right, depth, weights):
    lane = lane_of(own[0].shape)
    totals = [jnp.zeros_like(own[0]) for _ in own]
    for o, w in zip((-1, 0, 1, 2), weights):
        s = depth + o
        t = lane + s
        shift = (s + LANES) & (LANES - 1)
        for n in range(len(own)):
            x = jnp.where(t <= LANES - 1, own[n], left[n])
            if o == -1:
                x = jnp.where(t == -1, right[n], x)
            totals[n] = totals[n] + w * pltpu.roll(x, shift, axis=1)
    return totals


def depart_beside(own, left, right, depth, weights):
    lane = lane_of(own[0].shape)
    totals = [jnp.zeros_like(own[0]) for _ in own]
    for o, w in zip((-1, 0, 1, 2), weights):
        s = depth + o
        t = lane + s
        shift = (s + LANES) & (LANES - 1)
        for n in range(len(own)):
            x = jnp.where(t <= LANES - 1, left[n], own[n])
            if o < 2:
                x = jnp.where((t >= 0) & (t <= 1), right[n], x)
            if o == -1:
                x = jnp.where(t == -1, own[n], x)
            totals[n] = totals[n] + w * pltpu.roll(x, shift, axis=1)
    return totals


def beside_pair(own, halo):
    lane = lane_of(own.shape)
    first, last = lane == 0, lane == LANES - 1
    return (
        (turn(jnp.where(first, halo, own), -1), turn(jnp.where(last, halo, own), 1)),
        (turn(jnp.where(first, own, halo), -1), turn(jnp.where(last, own, halo), 1)),
    )


def update(lev, clat, depth_ref, fields, frac, helm, main, edge, above, below, la, lb, ra, rb,
           departed, pressure, ext, hel, rhs_s, p1_s):
    bands = clat // BAND
    j = lax.axis_index("lat")
    inside = (j > 0, j < lax.axis_size("lat") - 1)
    jet = jet_band(depth_ref, bands)
    lane = lane_of((BAND, LANES))
    for k in range(lev):
        for b in range(bands):
            rows = pl.ds(b * BAND, BAND)
            depth = depth_ref[b * BAND]
            slot = b - (b > jet).astype(jnp.int32)
            amount = (2 * LANES - NEAR - NEAR * slot) & (LANES - 1)
            whole = b == jet
            own = [fields[f, k, rows, :] for f in range(5)]
            left = [jnp.where(whole, main[0, f, k], pltpu.roll(main[1, f, k], amount, axis=1)) for f in range(5)]
            right = [turn(edge[k], -(32 * b + 3 * f)) for f in range(5)]
            got = depart(own, left, right, depth, interp_weights(frac[k, rows, :]))
            for f in range(5):
                departed[f, k, rows, :] = got[f]
            fr = jnp.where(lane < 64, turn(edge[k], -(32 * b + 15)), turn(main[1, 0, k], 18 - 3 * b))
            he = jnp.where(lane < 64, turn(edge[k], -(32 * b + 17)), turn(main[1, 0, k], 17 - 3 * b))
            pick = lambda z: [z[f] for f in HALO_FIELDS]
            past = depart_beside(pick(own), pick(left), pick(right), depth, interp_weights(fr))
            at = pl.ds((b + 1) * BAND, BAND)
            for q, f in enumerate(HALO_FIELDS):
                ext[q, 0, k, at, :] = got[f]
                ext[q, 1, k, at, :] = past[q]
            hel[0, k, at, :] = helm[k, rows, :]
            hel[1, k, at, :] = he
    for side, (mine, diag, thin) in enumerate(((above, la, ra), (below, lb, rb))):
        depth = jnp.max(mine[5]).astype(jnp.int32)
        own = [mine[q] for q in range(3)]
        left = [diag[q] for q in range(3)]
        g = thin[...]
        right = [turn(g, -3 * q) for q in range(3)]
        fr = jnp.where(lane < 64, turn(g, -9), turn(left[0], -2))
        he = jnp.where(lane < 64, turn(g, -11), turn(left[0], -3))
        got = depart(own, left, right, depth, interp_weights(mine[3]))
        past = depart_beside(own, left, right, depth, interp_weights(fr))
        at = BAND - 2 if side == 0 else BAND + clat
        for k in range(lev):
            pair = slice(2 * k, 2 * k + 2)
            for q in range(3):
                ext[q, 0, k, at:at + 2, :] = jnp.where(inside[side], got[q], 0.0)[pair]
                ext[q, 1, k, at:at + 2, :] = jnp.where(inside[side], past[q], 0.0)[pair]
            hel[0, k, at:at + 2, :] = mine[4][pair]
            hel[1, k, at:at + 2, :] = he[pair]
    tall = clat + BAND
    row = lax.broadcasted_iota(jnp.int32, (tall, LANES), 0)
    outside = ((row == 0) & jnp.logical_not(inside[0])) | ((row == clat + 1) & jnp.logical_not(inside[1]))
    first = BAND - 1
    for k in range(lev):
        mid = pl.ds(first, tall)
        up, down = pl.ds(first - 1, tall), pl.ds(first + 1, tall)
        u_all = beside_pair(ext[0, 0, k, mid, :], ext[0, 1, k, mid, :])
        phi = [ext[2, h, k, mid, :] for h in range(2)]
        phi_all = beside_pair(*phi)
        for h in range(2):
            div = 0.5 * (u_all[h][0] - u_all[h][1] + ext[1, h, k, down, :] - ext[1, h, k, up, :])
            rhs = phi[h] - 0.5 * div
            around = phi_all[h][0] + phi_all[h][1] + ext[2, h, k, down, :] + ext[2, h, k, up, :]
            p1 = (rhs + around) / (4.0 + hel[h, k, mid, :])
            p1_s[h, k] = jnp.where(outside, 0.0, p1)
            if h == 0:
                rhs_s[k] = rhs
        mid = pl.ds(1, clat)
        east, west = beside_pair(p1_s[0, k, mid, :], p1_s[1, k, mid, :])[0]
        around = east + west + p1_s[0, k, pl.ds(2, clat), :] + p1_s[0, k, pl.ds(0, clat), :]
        pressure[k] = (rhs_s[k, mid, :] + around) / (4.0 + helm[k])


def local(fields, depth, frac, helm):
    lev, clat, clon = fields.shape[1:]
    nothing = pl.BlockSpec(memory_space=pl.ANY)
    vmem = pl.BlockSpec(memory_space=pltpu.VMEM)
    smem = pl.BlockSpec(memory_space=pltpu.SMEM)
    tiles = [(2, 5, lev, BAND, clon), (lev, BAND, clon), (6, 2 * lev, clon), (6, 2 * lev, clon),
             (3, 2 * lev, clon), (3, 2 * lev, clon), (2 * lev, clon), (2 * lev, clon)]
    halos = pl.pallas_call(
        functools.partial(exchange, lev, clat),
        out_shape=[jax.ShapeDtypeStruct(t, F32) for t in tiles],
        in_specs=[smem, nothing, nothing, nothing],
        out_specs=[nothing] * len(tiles),
        scratch_shapes=[
            pltpu.VMEM(fields.shape, F32), pltpu.VMEM(frac.shape, F32), pltpu.VMEM(helm.shape, F32),
            *[pltpu.VMEM(t, F32) for t in tiles],
            pltpu.SemaphoreType.DMA((3,)),
            pltpu.SemaphoreType.DMA((8,)),
            pltpu.SemaphoreType.DMA((8,)),
        ],
        compiler_params=pltpu.CompilerParams(collective_id=0, has_side_effects=True, vmem_limit_bytes=8 << 20),
        name="exchange",
    )(depth, fields, frac, helm)
    tall = clat + 2 * BAND
    return pl.pallas_call(
        functools.partial(update, lev, clat),
        out_shape=[jax.ShapeDtypeStruct(fields.shape, F32), jax.ShapeDtypeStruct(frac.shape, F32)],
        in_specs=[smem] + [vmem] * (3 + len(tiles)),
        out_specs=[vmem, vmem],
        scratch_shapes=[
            pltpu.VMEM((3, 2, lev, tall, clon), F32),
            pltpu.VMEM((2, lev, tall, clon), F32),
            pltpu.VMEM((lev, clat + BAND, clon), F32),
            pltpu.VMEM((2, lev, clat + BAND, clon), F32),
        ],
        compiler_params=pltpu.CompilerParams(vmem_limit_bytes=8 << 20),
        name="update",
    )(depth, fields, frac, helm, *halos)


def solution(mesh):
    placed = (P(None, None, "lat", "lon"), P("lat"), P(None, "lat", "lon"), P(None, "lat", "lon"))
    return jax.shard_map(
        local,
        mesh=mesh,
        in_specs=placed,
        out_specs=(P(None, None, "lat", "lon"), P(None, "lat", "lon")),
        check_vma=False,
    )
```

```python
import functools

import jax
import jax.numpy as jnp
from jax import lax
from jax.experimental import pallas as pl
from jax.experimental.pallas import tpu as pltpu
from jax.sharding import PartitionSpec as P

BAND = 8
SHALLOW = 32
LANES = 128
NEAR = SHALLOW + 4
F32 = jnp.float32
MESH = pl.DeviceIdType.MESH
HALO_FIELDS = (0, 1, 3)
SPARE = 108


def turn(x, shift):
    shift %= LANES
    return x if shift == 0 else pltpu.roll(x, shift, axis=1)


def lane_of(shape):
    return lax.broadcasted_iota(jnp.int32, shape, len(shape) - 1)


def jet_band(depth_ref, bands):
    jet = jnp.int32(0)
    for b in range(1, bands):
        jet = jnp.where(depth_ref[b * BAND] > SHALLOW, b, jet)
    return jet


def exchange(lev, clat, depth_hbm, fields_hbm, frac_hbm, helm_hbm,
             main_o, edge_o, above_o, below_o, la_o, lb_o, ra_o, rb_o,
             depth_ref, fields, frac, helm, main, edge, top, bottom, dtop, dbottom, gtop, gbottom,
             in_sem, send_sem, recv_sem):
    bands = clat // BAND
    loads = [
        pltpu.make_async_copy(src, dst, in_sem.at[i])
        for i, (src, dst) in enumerate(
            ((depth_hbm, depth_ref), (fields_hbm, fields), (frac_hbm, frac), (helm_hbm, helm)))
    ]
    for load in loads:
        load.start()
    nlon, nlat = lax.axis_size("lon"), lax.axis_size("lat")
    i, j = lax.axis_index("lon"), lax.axis_index("lat")
    east, west = lax.rem(i + 1, nlon), lax.rem(i + nlon - 1, nlon)
    south, north = lax.rem(j + 1, nlat), lax.rem(j + nlat - 1, nlat)
    peers = [{"lon": a, "lat": b} for a, b in (
        (east, j), (west, j), (i, north), (i, south),
        (east, north), (east, south), (west, north), (west, south))]
    barrier = pltpu.get_barrier_semaphore()
    for peer in peers:
        pl.semaphore_signal(barrier, inc=1, device_id=peer, device_id_type=MESH)

    def copy(n, src, dst, peer):
        return pltpu.make_async_remote_copy(
            src_ref=src, dst_ref=dst, send_sem=send_sem.at[n], recv_sem=recv_sem.at[n],
            device_id=peers[peer], device_id_type=MESH)

    copies = [
        copy(0, main, main_o, 0),
        copy(1, edge, edge_o, 1),
        copy(2, top, below_o, 2),
        copy(3, bottom, above_o, 3),
        copy(4, dtop, lb_o, 4),
        copy(5, dbottom, la_o, 5),
        copy(6, gtop, rb_o, 6),
        copy(7, gbottom, ra_o, 7),
    ]
    for load in loads:
        load.wait()
    jet = jet_band(depth_ref, bands)
    nf = 5 * lev * BAND
    lane = lane_of((nf, LANES))
    jet = jnp.full((nf, LANES), jet)
    x = [fields[:, :, pl.ds(b * BAND, BAND), :].reshape(nf, LANES) for b in range(bands)]
    whole = x[0]
    for b in range(1, bands):
        whole = jnp.where(jet == b, x[b], whole)
    main[0] = whole.reshape(5, lev, BAND, LANES)
    packed = None
    for slot in range(bands - 1):
        y = jnp.where(jet > slot, x[slot], x[slot + 1])
        y = turn(y, slot * NEAR + NEAR - LANES)
        packed = y if packed is None else jnp.where(lane >= slot * NEAR, y, packed)
    main[1] = packed.reshape(5, lev, BAND, LANES)
    nk = lev * BAND
    lane = lane_of((nk, LANES))
    rest = main[1, 0].reshape(nk, LANES)
    for b in range(bands):
        at = SPARE + 3 * b
        rows = pl.ds(b * BAND, BAND)
        fr = turn(frac[:, rows, :].reshape(nk, LANES), at - (LANES - 2))
        he = turn(helm[:, rows, :].reshape(nk, LANES), at + 2 - (LANES - 1))
        rest = jnp.where((lane >= at) & (lane < at + 2), fr, rest)
        rest = jnp.where(lane == at + 2, he, rest)
    main[1, 0] = rest.reshape(lev, BAND, LANES)
    pl.semaphore_wait(barrier, len(peers))
    copies[0].start()

    acc = jnp.zeros((nk, LANES), F32)
    for b in range(bands):
        rows = pl.ds(b * BAND, BAND)
        for n in range(7):
            src = fields[n, :, rows, :] if n < 5 else (frac if n == 5 else helm)[:, rows, :]
            at = 32 * b + (17 if n == 6 else 3 * n)
            wide = 3 if n < 5 else 7 - n
            acc = jnp.where((lane >= at) & (lane < at + wide), turn(src.reshape(nk, LANES), at), acc)
    edge[...] = acc.reshape(lev, BAND, LANES)
    copies[1].start()

    lane8 = lane_of((2 * lev, LANES))
    for row, mine, diag, thin, n, at_depth in (
            (0, top, dtop, gtop, 0, 0), (clat - 2, bottom, dbottom, gbottom, 1, clat - 1)):
        for q in range(5):
            src = fields.at[HALO_FIELDS[q]] if q < 3 else (frac if q == 3 else helm)
            for k in range(lev):
                mine[q, 2 * k:2 * k + 2, :] = src[k, row:row + 2, :]
        mine[5] = jnp.full((2 * lev, LANES), depth_ref[at_depth].astype(F32))
        copies[2 + n].start()
        u = jnp.where(lane8 < 2, turn(mine[3], 2), mine[0])
        diag[0] = jnp.where(lane8 == 2, turn(mine[4], 3), u)
        diag[1] = mine[1]
        diag[2] = mine[2]
        copies[4 + n].start()
        g = mine[0]
        for q in range(1, 5):
            at = 11 if q == 4 else 3 * q
            g = jnp.where(lane8 >= at, turn(mine[q], at), g)
        thin[...] = g
        copies[6 + n].start()
    for c in copies:
        c.wait()


def interp_weights(frac):
    s = -frac
    return [
        s * (s + 1.0) * (s + 2.0) / 6.0,
        -(s - 1.0) * (s + 1.0) * (s + 2.0) / 2.0,
        (s - 1.0) * s * (s + 2.0) / 2.0,
        -(s - 1.0) * s * (s + 1.0) / 6.0,
    ]


def depart(own, left, right, depth, weights):
    lane = lane_of(own[0].shape)
    totals = [jnp.zeros_like(own[0]) for _ in own]
    for o, w in zip((-1, 0, 1, 2), weights):
        s = depth + o
        t = lane + s
        shift = (s + LANES) & (LANES - 1)
        for n in range(len(own)):
            x = jnp.where(t <= LANES - 1, own[n], left[n])
            if o == -1:
                x = jnp.where(t == -1, right[n], x)
            totals[n] = totals[n] + w * pltpu.roll(x, shift, axis=1)
    return totals


def depart_beside(own, left, right, depth, weights):
    lane = lane_of(own[0].shape)
    totals = [jnp.zeros_like(own[0]) for _ in own]
    for o, w in zip((-1, 0, 1, 2), weights):
        s = depth + o
        t = lane + s
        shift = (s + LANES) & (LANES - 1)
        for n in range(len(own)):
            x = jnp.where(t <= LANES - 1, left[n], own[n])
            if o < 2:
                x = jnp.where((t >= 0) & (t <= 1), right[n], x)
            if o == -1:
                x = jnp.where(t == -1, own[n], x)
            totals[n] = totals[n] + w * pltpu.roll(x, shift, axis=1)
    return totals


def beside_pair(own, halo):
    lane = lane_of(own.shape)
    first, last = lane == 0, lane == LANES - 1
    return (
        (turn(jnp.where(first, halo, own), -1), turn(jnp.where(last, halo, own), 1)),
        (turn(jnp.where(first, own, halo), -1), turn(jnp.where(last, own, halo), 1)),
    )


def update(lev, clat, *refs):
    sources, (departed_o, pressure_o), (ext, hel, rhs_s, p1_s), here, (departed, pressure), (in_sem, out_sem) = (
        refs[:12], refs[12:14], refs[14:18], refs[18:30], refs[30:32], refs[32:])
    loads = [pltpu.make_async_copy(src, dst, in_sem.at[n]) for n, (src, dst) in enumerate(zip(sources, here))]
    for load in loads:
        load.start()
    depth_ref, fields, frac, helm, main, edge, above, below, la, lb, ra, rb = here
    bands = clat // BAND
    for load in loads:
        load.wait()
    stores = []
    j = lax.axis_index("lat")
    inside = (j > 0, j < lax.axis_size("lat") - 1)
    jet = jet_band(depth_ref, bands)
    lane = lane_of((BAND, LANES))
    for k in range(lev):
        for b in range(bands):
            rows = pl.ds(b * BAND, BAND)
            depth = depth_ref[b * BAND]
            slot = b - (b > jet).astype(jnp.int32)
            amount = (2 * LANES - NEAR - NEAR * slot) & (LANES - 1)
            whole = b == jet
            own = [fields[f, k, rows, :] for f in range(5)]
            left = [jnp.where(whole, main[0, f, k], pltpu.roll(main[1, f, k], amount, axis=1)) for f in range(5)]
            right = [turn(edge[k], -(32 * b + 3 * f)) for f in range(5)]
            got = depart(own, left, right, depth, interp_weights(frac[k, rows, :]))
            for f in range(5):
                departed[f, k, rows, :] = got[f]
            fr = jnp.where(lane < 64, turn(edge[k], -(32 * b + 15)), turn(main[1, 0, k], 18 - 3 * b))
            he = jnp.where(lane < 64, turn(edge[k], -(32 * b + 17)), turn(main[1, 0, k], 17 - 3 * b))
            pick = lambda z: [z[f] for f in HALO_FIELDS]
            past = depart_beside(pick(own), pick(left), pick(right), depth, interp_weights(fr))
            at = pl.ds((b + 1) * BAND, BAND)
            for q, f in enumerate(HALO_FIELDS):
                ext[q, 0, k, at, :] = got[f]
                ext[q, 1, k, at, :] = past[q]
            hel[0, k, at, :] = helm[k, rows, :]
            hel[1, k, at, :] = he
        stores.append(pltpu.make_async_copy(departed.at[:, k], departed_o.at[:, k], out_sem.at[k]))
        stores[-1].start()
    for side, (mine, diag, thin) in enumerate(((above, la, ra), (below, lb, rb))):
        depth = jnp.max(mine[5]).astype(jnp.int32)
        own = [mine[q] for q in range(3)]
        left = [diag[q] for q in range(3)]
        g = thin[...]
        right = [turn(g, -3 * q) for q in range(3)]
        fr = jnp.where(lane < 64, turn(g, -9), turn(left[0], -2))
        he = jnp.where(lane < 64, turn(g, -11), turn(left[0], -3))
        got = depart(own, left, right, depth, interp_weights(mine[3]))
        past = depart_beside(own, left, right, depth, interp_weights(fr))
        at = BAND - 2 if side == 0 else BAND + clat
        for k in range(lev):
            pair = slice(2 * k, 2 * k + 2)
            for q in range(3):
                ext[q, 0, k, at:at + 2, :] = jnp.where(inside[side], got[q], 0.0)[pair]
                ext[q, 1, k, at:at + 2, :] = jnp.where(inside[side], past[q], 0.0)[pair]
            hel[0, k, at:at + 2, :] = mine[4][pair]
            hel[1, k, at:at + 2, :] = he[pair]
    tall = clat + BAND
    row = lax.broadcasted_iota(jnp.int32, (tall, LANES), 0)
    outside = ((row == 0) & jnp.logical_not(inside[0])) | ((row == clat + 1) & jnp.logical_not(inside[1]))
    first = BAND - 1
    for k in range(lev):
        mid = pl.ds(first, tall)
        up, down = pl.ds(first - 1, tall), pl.ds(first + 1, tall)
        u_all = beside_pair(ext[0, 0, k, mid, :], ext[0, 1, k, mid, :])
        phi = [ext[2, h, k, mid, :] for h in range(2)]
        phi_all = beside_pair(*phi)
        for h in range(2):
            div = 0.5 * (u_all[h][0] - u_all[h][1] + ext[1, h, k, down, :] - ext[1, h, k, up, :])
            rhs = phi[h] - 0.5 * div
            around = phi_all[h][0] + phi_all[h][1] + ext[2, h, k, down, :] + ext[2, h, k, up, :]
            p1 = (rhs + around) / (4.0 + hel[h, k, mid, :])
            p1_s[h, k] = jnp.where(outside, 0.0, p1)
            if h == 0:
                rhs_s[k] = rhs
        mid = pl.ds(1, clat)
        east, west = beside_pair(p1_s[0, k, mid, :], p1_s[1, k, mid, :])[0]
        around = east + west + p1_s[0, k, pl.ds(2, clat), :] + p1_s[0, k, pl.ds(0, clat), :]
        pressure[k] = (rhs_s[k, mid, :] + around) / (4.0 + helm[k])
    stores.append(pltpu.make_async_copy(pressure, pressure_o, out_sem.at[lev]))
    stores[-1].start()
    for store in stores:
        store.wait()


def local(fields, depth, frac, helm):
    lev, clat, clon = fields.shape[1:]
    hbm = pl.BlockSpec(memory_space=pltpu.HBM)
    tiles = [(2, 5, lev, BAND, clon), (lev, BAND, clon), (6, 2 * lev, clon), (6, 2 * lev, clon),
             (3, 2 * lev, clon), (3, 2 * lev, clon), (2 * lev, clon), (2 * lev, clon)]
    halos = pl.pallas_call(
        functools.partial(exchange, lev, clat),
        out_shape=[jax.ShapeDtypeStruct(t, F32) for t in tiles],
        in_specs=[hbm] * 4,
        out_specs=[hbm] * len(tiles),
        scratch_shapes=[
            pltpu.SMEM(depth.shape, jnp.int32),
            pltpu.VMEM(fields.shape, F32), pltpu.VMEM(frac.shape, F32), pltpu.VMEM(helm.shape, F32),
            *[pltpu.VMEM(t, F32) for t in tiles],
            pltpu.SemaphoreType.DMA((4,)),
            pltpu.SemaphoreType.DMA((8,)),
            pltpu.SemaphoreType.DMA((8,)),
        ],
        compiler_params=pltpu.CompilerParams(collective_id=0, has_side_effects=True, vmem_limit_bytes=60 << 20),
        name="exchange",
    )(depth, fields, frac, helm)
    tall = clat + 2 * BAND
    return pl.pallas_call(
        functools.partial(update, lev, clat),
        out_shape=[jax.ShapeDtypeStruct(fields.shape, F32), jax.ShapeDtypeStruct(frac.shape, F32)],
        in_specs=[hbm] * (4 + len(tiles)),
        out_specs=[hbm, hbm],
        scratch_shapes=[
            pltpu.VMEM((3, 2, lev, tall, clon), F32),
            pltpu.VMEM((2, lev, tall, clon), F32),
            pltpu.VMEM((lev, clat + BAND, clon), F32),
            pltpu.VMEM((2, lev, clat + BAND, clon), F32),
            pltpu.SMEM(depth.shape, jnp.int32),
            *[pltpu.VMEM(t, F32) for t in (fields.shape, frac.shape, helm.shape, *tiles, fields.shape, frac.shape)],
            pltpu.SemaphoreType.DMA((4 + len(tiles),)),
            pltpu.SemaphoreType.DMA((lev + 1,)),
        ],
        compiler_params=pltpu.CompilerParams(vmem_limit_bytes=60 << 20),
        name="update",
    )(depth, fields, frac, helm, *halos)


def solution(mesh):
    placed = (P(None, None, "lat", "lon"), P("lat"), P(None, "lat", "lon"), P(None, "lat", "lon"))
    return jax.shard_map(
        local,
        mesh=mesh,
        in_specs=placed,
        out_specs=(P(None, None, "lat", "lon"), P(None, "lat", "lon")),
        check_vma=False,
    )
```

```python
import functools

import jax
import jax.numpy as jnp
from jax import lax
from jax.experimental import pallas as pl
from jax.experimental.pallas import tpu as pltpu
from jax.sharding import PartitionSpec as P

BAND = 8
SHALLOW = 32
LANES = 128
NEAR = SHALLOW + 4
F32 = jnp.float32
MESH = pl.DeviceIdType.MESH
HALO_FIELDS = (0, 1, 3)
SPARE = 108


def turn(x, shift):
    shift %= LANES
    return x if shift == 0 else pltpu.roll(x, shift, axis=1)


def lane_of(shape):
    return lax.broadcasted_iota(jnp.int32, shape, len(shape) - 1)


def jet_band(depth_ref, bands):
    jet = jnp.int32(0)
    for b in range(1, bands):
        jet = jnp.where(depth_ref[b * BAND] > SHALLOW, b, jet)
    return jet


def exchange(lev, clat, depth_hbm, fields_hbm, frac_hbm, helm_hbm,
             main_o, edge_o, above_o, below_o, la_o, lb_o, ra_o, rb_o,
             depth_ref, fields, frac, helm, main, edge, top, bottom, dtop, dbottom, gtop, gbottom,
             in_sem, send_sem, recv_sem):
    bands = clat // BAND
    loads = [
        pltpu.make_async_copy(src, dst, in_sem.at[i])
        for i, (src, dst) in enumerate(
            ((depth_hbm, depth_ref), (fields_hbm, fields), (frac_hbm, frac), (helm_hbm, helm)))
    ]
    for load in loads:
        load.start()
    nlon, nlat = lax.axis_size("lon"), lax.axis_size("lat")
    i, j = lax.axis_index("lon"), lax.axis_index("lat")
    east, west = lax.rem(i + 1, nlon), lax.rem(i + nlon - 1, nlon)
    south, north = lax.rem(j + 1, nlat), lax.rem(j + nlat - 1, nlat)
    peers = [{"lon": a, "lat": b} for a, b in (
        (east, j), (west, j), (i, north), (i, south),
        (east, north), (east, south), (west, north), (west, south))]
    barrier = pltpu.get_barrier_semaphore()
    for peer in peers:
        pl.semaphore_signal(barrier, inc=1, device_id=peer, device_id_type=MESH)

    def copy(n, src, dst, peer):
        return pltpu.make_async_remote_copy(
            src_ref=src, dst_ref=dst, send_sem=send_sem.at[n], recv_sem=recv_sem.at[n],
            device_id=peers[peer], device_id_type=MESH)

    copies = [
        copy(0, main.at[0], main_o.at[0], 0),
        copy(1, edge, edge_o, 1),
        copy(2, top, below_o, 2),
        copy(3, bottom, above_o, 3),
        copy(4, dtop, lb_o, 4),
        copy(5, dbottom, la_o, 5),
        copy(6, gtop, rb_o, 6),
        copy(7, gbottom, ra_o, 7),
        copy(8, main.at[1], main_o.at[1], 0),
    ]
    for load in loads:
        load.wait()
    jet = jet_band(depth_ref, bands)
    nf = 5 * lev * BAND
    lane = lane_of((nf, LANES))
    jet = jnp.full((nf, LANES), jet)
    x = [fields[:, :, pl.ds(b * BAND, BAND), :].reshape(nf, LANES) for b in range(bands)]
    whole = x[0]
    for b in range(1, bands):
        whole = jnp.where(jet == b, x[b], whole)
    main[0] = whole.reshape(5, lev, BAND, LANES)
    pl.semaphore_wait(barrier, len(peers))
    copies[0].start()
    packed = None
    for slot in range(bands - 1):
        y = jnp.where(jet > slot, x[slot], x[slot + 1])
        y = turn(y, slot * NEAR + NEAR - LANES)
        packed = y if packed is None else jnp.where(lane >= slot * NEAR, y, packed)
    main[1] = packed.reshape(5, lev, BAND, LANES)
    nk = lev * BAND
    lane = lane_of((nk, LANES))
    rest = main[1, 0].reshape(nk, LANES)
    for b in range(bands):
        at = SPARE + 3 * b
        rows = pl.ds(b * BAND, BAND)
        fr = turn(frac[:, rows, :].reshape(nk, LANES), at - (LANES - 2))
        he = turn(helm[:, rows, :].reshape(nk, LANES), at + 2 - (LANES - 1))
        rest = jnp.where((lane >= at) & (lane < at + 2), fr, rest)
        rest = jnp.where(lane == at + 2, he, rest)
    main[1, 0] = rest.reshape(lev, BAND, LANES)
    copies[8].start()

    acc = jnp.zeros((nk, LANES), F32)
    for b in range(bands):
        rows = pl.ds(b * BAND, BAND)
        for n in range(7):
            src = fields[n, :, rows, :] if n < 5 else (frac if n == 5 else helm)[:, rows, :]
            at = 32 * b + (17 if n == 6 else 3 * n)
            wide = 3 if n < 5 else 7 - n
            acc = jnp.where((lane >= at) & (lane < at + wide), turn(src.reshape(nk, LANES), at), acc)
    edge[...] = acc.reshape(lev, BAND, LANES)
    copies[1].start()

    lane8 = lane_of((2 * lev, LANES))
    for row, mine, diag, thin, n, at_depth in (
            (0, top, dtop, gtop, 0, 0), (clat - 2, bottom, dbottom, gbottom, 1, clat - 1)):
        for q in range(5):
            src = fields.at[HALO_FIELDS[q]] if q < 3 else (frac if q == 3 else helm)
            for k in range(lev):
                mine[q, 2 * k:2 * k + 2, :] = src[k, row:row + 2, :]
        mine[5] = jnp.full((2 * lev, LANES), depth_ref[at_depth].astype(F32))
        copies[2 + n].start()
        u = jnp.where(lane8 < 2, turn(mine[3], 2), mine[0])
        diag[0] = jnp.where(lane8 == 2, turn(mine[4], 3), u)
        diag[1] = mine[1]
        diag[2] = mine[2]
        copies[4 + n].start()
        g = mine[0]
        for q in range(1, 5):
            at = 11 if q == 4 else 3 * q
            g = jnp.where(lane8 >= at, turn(mine[q], at), g)
        thin[...] = g
        copies[6 + n].start()
    for c in copies:
        c.wait()


def interp_weights(frac):
    s = -frac
    below, above = (s - 1.0) * s, (s + 1.0) * (s + 2.0)
    return [
        s * above * (1.0 / 6.0),
        (s - 1.0) * above * -0.5,
        below * (s + 2.0) * 0.5,
        below * (s + 1.0) * (-1.0 / 6.0),
    ]


def depart(own, left, right, depth, weights):
    lane = lane_of(own[0].shape)
    totals = [jnp.zeros_like(own[0]) for _ in own]
    for o, w in zip((-1, 0, 1, 2), weights):
        s = depth + o
        t = lane + s
        shift = (s + LANES) & (LANES - 1)
        for n in range(len(own)):
            x = jnp.where(t <= LANES - 1, own[n], left[n])
            if o == -1:
                x = jnp.where(t == -1, right[n], x)
            totals[n] = totals[n] + w * pltpu.roll(x, shift, axis=1)
    return totals


def depart_beside(own, left, right, depth, weights):
    lane = lane_of(own[0].shape)
    totals = [jnp.zeros_like(own[0]) for _ in own]
    for o, w in zip((-1, 0, 1, 2), weights):
        s = depth + o
        t = lane + s
        shift = (s + LANES) & (LANES - 1)
        for n in range(len(own)):
            x = jnp.where(t <= LANES - 1, left[n], own[n])
            if o < 2:
                x = jnp.where((t >= 0) & (t <= 1), right[n], x)
            if o == -1:
                x = jnp.where(t == -1, own[n], x)
            totals[n] = totals[n] + w * pltpu.roll(x, shift, axis=1)
    return totals


def beside_pair(own, halo):
    lane = lane_of(own.shape)
    first, last = lane == 0, lane == LANES - 1
    return (
        (turn(jnp.where(first, halo, own), -1), turn(jnp.where(last, halo, own), 1)),
        (turn(jnp.where(first, own, halo), -1), turn(jnp.where(last, own, halo), 1)),
    )


def update(lev, clat, *refs):
    sources, (departed_o, pressure_o), (ext, hel, rhs_s, p1_s, wts), here, (departed, pressure), (in_sem, out_sem) = (
        refs[:12], refs[12:14], refs[14:19], refs[19:31], refs[31:33], refs[33:])
    loads = [pltpu.make_async_copy(src, dst, in_sem.at[n]) for n, (src, dst) in enumerate(zip(sources, here))]
    for n in (2, 0, 1, *range(3, len(loads))):
        loads[n].start()
    depth_ref, fields, frac, helm, main, edge, above, below, la, lb, ra, rb = here
    bands = clat // BAND
    loads.pop(2).wait()
    for k in range(lev):
        for o, w in enumerate(interp_weights(frac[k])):
            wts[o, k] = w
    for load in loads:
        load.wait()
    stores = []
    j = lax.axis_index("lat")
    inside = (j > 0, j < lax.axis_size("lat") - 1)
    jet = jet_band(depth_ref, bands)
    lane = lane_of((BAND, LANES))
    for k in range(lev):
        for b in range(bands):
            rows = pl.ds(b * BAND, BAND)
            depth = depth_ref[b * BAND]
            slot = b - (b > jet).astype(jnp.int32)
            amount = (2 * LANES - NEAR - NEAR * slot) & (LANES - 1)
            whole = b == jet
            own = [fields[f, k, rows, :] for f in range(5)]
            left = [jnp.where(whole, main[0, f, k], pltpu.roll(main[1, f, k], amount, axis=1)) for f in range(5)]
            right = [turn(edge[k], -(32 * b + 3 * f)) for f in range(5)]
            got = depart(own, left, right, depth, [wts[o, k, rows, :] for o in range(4)])
            for f in range(5):
                departed[f, k, rows, :] = got[f]
            fr = jnp.where(lane < 64, turn(edge[k], -(32 * b + 15)), turn(main[1, 0, k], 18 - 3 * b))
            he = jnp.where(lane < 64, turn(edge[k], -(32 * b + 17)), turn(main[1, 0, k], 17 - 3 * b))
            pick = lambda z: [z[f] for f in HALO_FIELDS]
            past = depart_beside(pick(own), pick(left), pick(right), depth, interp_weights(fr))
            at = pl.ds((b + 1) * BAND, BAND)
            for q, f in enumerate(HALO_FIELDS):
                ext[q, 0, k, at, :] = got[f]
                ext[q, 1, k, at, :] = past[q]
            hel[0, k, at, :] = helm[k, rows, :]
            hel[1, k, at, :] = he
        stores.append(pltpu.make_async_copy(departed.at[:, k], departed_o.at[:, k], out_sem.at[k]))
        stores[-1].start()
    for side, (mine, diag, thin) in enumerate(((above, la, ra), (below, lb, rb))):
        depth = jnp.max(mine[5]).astype(jnp.int32)
        own = [mine[q] for q in range(3)]
        left = [diag[q] for q in range(3)]
        g = thin[...]
        right = [turn(g, -3 * q) for q in range(3)]
        fr = jnp.where(lane < 64, turn(g, -9), turn(left[0], -2))
        he = jnp.where(lane < 64, turn(g, -11), turn(left[0], -3))
        got = depart(own, left, right, depth, interp_weights(mine[3]))
        past = depart_beside(own, left, right, depth, interp_weights(fr))
        at = BAND - 2 if side == 0 else BAND + clat
        for k in range(lev):
            pair = slice(2 * k, 2 * k + 2)
            for q in range(3):
                ext[q, 0, k, at:at + 2, :] = jnp.where(inside[side], got[q], 0.0)[pair]
                ext[q, 1, k, at:at + 2, :] = jnp.where(inside[side], past[q], 0.0)[pair]
            hel[0, k, at:at + 2, :] = mine[4][pair]
            hel[1, k, at:at + 2, :] = he[pair]
    tall = clat + BAND
    row = lax.broadcasted_iota(jnp.int32, (tall, LANES), 0)
    outside = ((row == 0) & jnp.logical_not(inside[0])) | ((row == clat + 1) & jnp.logical_not(inside[1]))
    first = BAND - 1
    for k in range(lev):
        mid = pl.ds(first, tall)
        up, down = pl.ds(first - 1, tall), pl.ds(first + 1, tall)
        u_all = beside_pair(ext[0, 0, k, mid, :], ext[0, 1, k, mid, :])
        phi = [ext[2, h, k, mid, :] for h in range(2)]
        phi_all = beside_pair(*phi)
        for h in range(2):
            div = 0.5 * (u_all[h][0] - u_all[h][1] + ext[1, h, k, down, :] - ext[1, h, k, up, :])
            rhs = phi[h] - 0.5 * div
            around = phi_all[h][0] + phi_all[h][1] + ext[2, h, k, down, :] + ext[2, h, k, up, :]
            p1 = (rhs + around) / (4.0 + hel[h, k, mid, :])
            p1_s[h, k] = jnp.where(outside, 0.0, p1)
            if h == 0:
                rhs_s[k] = rhs
        mid = pl.ds(1, clat)
        east, west = beside_pair(p1_s[0, k, mid, :], p1_s[1, k, mid, :])[0]
        around = east + west + p1_s[0, k, pl.ds(2, clat), :] + p1_s[0, k, pl.ds(0, clat), :]
        pressure[k] = (rhs_s[k, mid, :] + around) / (4.0 + helm[k])
        stores.append(pltpu.make_async_copy(pressure.at[k], pressure_o.at[k], out_sem.at[lev + k]))
        stores[-1].start()
    for store in stores:
        store.wait()


def local(fields, depth, frac, helm):
    lev, clat, clon = fields.shape[1:]
    hbm = pl.BlockSpec(memory_space=pltpu.HBM)
    tiles = [(2, 5, lev, BAND, clon), (lev, BAND, clon), (6, 2 * lev, clon), (6, 2 * lev, clon),
             (3, 2 * lev, clon), (3, 2 * lev, clon), (2 * lev, clon), (2 * lev, clon)]
    halos = pl.pallas_call(
        functools.partial(exchange, lev, clat),
        out_shape=[jax.ShapeDtypeStruct(t, F32) for t in tiles],
        in_specs=[hbm] * 4,
        out_specs=[hbm] * len(tiles),
        scratch_shapes=[
            pltpu.SMEM(depth.shape, jnp.int32),
            pltpu.VMEM(fields.shape, F32), pltpu.VMEM(frac.shape, F32), pltpu.VMEM(helm.shape, F32),
            *[pltpu.VMEM(t, F32) for t in tiles],
            pltpu.SemaphoreType.DMA((4,)),
            pltpu.SemaphoreType.DMA((9,)),
            pltpu.SemaphoreType.DMA((9,)),
        ],
        compiler_params=pltpu.CompilerParams(collective_id=0, has_side_effects=True, vmem_limit_bytes=60 << 20),
        name="exchange",
    )(depth, fields, frac, helm)
    tall = clat + 2 * BAND
    return pl.pallas_call(
        functools.partial(update, lev, clat),
        out_shape=[jax.ShapeDtypeStruct(fields.shape, F32), jax.ShapeDtypeStruct(frac.shape, F32)],
        in_specs=[hbm] * (4 + len(tiles)),
        out_specs=[hbm, hbm],
        scratch_shapes=[
            pltpu.VMEM((3, 2, lev, tall, clon), F32),
            pltpu.VMEM((2, lev, tall, clon), F32),
            pltpu.VMEM((lev, clat + BAND, clon), F32),
            pltpu.VMEM((2, lev, clat + BAND, clon), F32),
            pltpu.VMEM((4, *frac.shape), F32),
            pltpu.SMEM(depth.shape, jnp.int32),
            *[pltpu.VMEM(t, F32) for t in (fields.shape, frac.shape, helm.shape, *tiles, fields.shape, frac.shape)],
            pltpu.SemaphoreType.DMA((4 + len(tiles),)),
            pltpu.SemaphoreType.DMA((2 * lev,)),
        ],
        compiler_params=pltpu.CompilerParams(vmem_limit_bytes=60 << 20),
        name="update",
    )(depth, fields, frac, helm, *halos)


def solution(mesh):
    placed = (P(None, None, "lat", "lon"), P("lat"), P(None, "lat", "lon"), P(None, "lat", "lon"))
    return jax.shard_map(
        local,
        mesh=mesh,
        in_specs=placed,
        out_specs=(P(None, None, "lat", "lon"), P(None, "lat", "lon")),
        check_vma=False,
    )
```

```python
import functools

import jax
import jax.numpy as jnp
from jax import lax
from jax.experimental import pallas as pl
from jax.experimental.pallas import tpu as pltpu
from jax.sharding import PartitionSpec as P

BAND = 8
SHALLOW = 32
LANES = 128
NEAR = SHALLOW + 4
F32 = jnp.float32
MESH = pl.DeviceIdType.MESH
HALO_FIELDS = (0, 1, 3)
SPARE = 108


def turn(x, shift):
    shift %= LANES
    return x if shift == 0 else pltpu.roll(x, shift, axis=1)


def lane_of(shape):
    return lax.broadcasted_iota(jnp.int32, shape, len(shape) - 1)


def jet_band(depth_ref, bands):
    jet = jnp.int32(0)
    for b in range(1, bands):
        jet = jnp.where(depth_ref[b * BAND] > SHALLOW, b, jet)
    return jet


def exchange(lev, clat, depth_hbm, fields_hbm, frac_hbm, helm_hbm,
             main_o, edge_o, above_o, below_o, la_o, lb_o, ra_o, rb_o,
             depth_ref, fields, frac, helm, main, edge, top, bottom, dtop, dbottom, gtop, gbottom,
             in_sem, send_sem, recv_sem):
    bands = clat // BAND
    loads = [
        pltpu.make_async_copy(src, dst, in_sem.at[i])
        for i, (src, dst) in enumerate(
            ((depth_hbm, depth_ref), (fields_hbm, fields), (frac_hbm, frac), (helm_hbm, helm)))
    ]
    for load in loads:
        load.start()
    nlon, nlat = lax.axis_size("lon"), lax.axis_size("lat")
    i, j = lax.axis_index("lon"), lax.axis_index("lat")
    east, west = lax.rem(i + 1, nlon), lax.rem(i + nlon - 1, nlon)
    south, north = lax.rem(j + 1, nlat), lax.rem(j + nlat - 1, nlat)
    peers = [{"lon": a, "lat": b} for a, b in (
        (east, j), (west, j), (i, north), (i, south),
        (east, north), (east, south), (west, north), (west, south))]
    barrier = pltpu.get_barrier_semaphore()
    for peer in peers:
        pl.semaphore_signal(barrier, inc=1, device_id=peer, device_id_type=MESH)

    def copy(n, src, dst, peer):
        return pltpu.make_async_remote_copy(
            src_ref=src, dst_ref=dst, send_sem=send_sem.at[n], recv_sem=recv_sem.at[n],
            device_id=peers[peer], device_id_type=MESH)

    copies = [
        copy(0, main.at[0], main_o.at[0], 0),
        copy(1, edge, edge_o, 1),
        copy(2, top, below_o, 2),
        copy(3, bottom, above_o, 3),
        copy(4, dtop, lb_o, 4),
        copy(5, dbottom, la_o, 5),
        copy(6, gtop, rb_o, 6),
        copy(7, gbottom, ra_o, 7),
        copy(8, main.at[1], main_o.at[1], 0),
    ]
    for load in loads:
        load.wait()
    jet = jet_band(depth_ref, bands)
    nf = 5 * lev * BAND
    lane = lane_of((nf, LANES))
    jet = jnp.full((nf, LANES), jet)
    x = [fields[:, :, pl.ds(b * BAND, BAND), :].reshape(nf, LANES) for b in range(bands)]
    whole = x[0]
    for b in range(1, bands):
        whole = jnp.where(jet == b, x[b], whole)
    main[0] = whole.reshape(5, lev, BAND, LANES)
    pl.semaphore_wait(barrier, len(peers))
    copies[0].start()
    packed = None
    for slot in range(bands - 1):
        y = jnp.where(jet > slot, x[slot], x[slot + 1])
        y = turn(y, slot * NEAR + NEAR - LANES)
        packed = y if packed is None else jnp.where(lane >= slot * NEAR, y, packed)
    main[1] = packed.reshape(5, lev, BAND, LANES)
    nk = lev * BAND
    lane = lane_of((nk, LANES))
    rest = main[1, 0].reshape(nk, LANES)
    for b in range(bands):
        at = SPARE + 3 * b
        rows = pl.ds(b * BAND, BAND)
        fr = turn(frac[:, rows, :].reshape(nk, LANES), at - (LANES - 2))
        he = turn(helm[:, rows, :].reshape(nk, LANES), at + 2 - (LANES - 1))
        rest = jnp.where((lane >= at) & (lane < at + 2), fr, rest)
        rest = jnp.where(lane == at + 2, he, rest)
    main[1, 0] = rest.reshape(lev, BAND, LANES)
    copies[8].start()

    acc = jnp.zeros((nk, LANES), F32)
    for b in range(bands):
        rows = pl.ds(b * BAND, BAND)
        for n in range(7):
            src = fields[n, :, rows, :] if n < 5 else (frac if n == 5 else helm)[:, rows, :]
            at = 32 * b + (17 if n == 6 else 3 * n)
            wide = 3 if n < 5 else 7 - n
            acc = jnp.where((lane >= at) & (lane < at + wide), turn(src.reshape(nk, LANES), at), acc)
    edge[...] = acc.reshape(lev, BAND, LANES)
    copies[1].start()

    lane8 = lane_of((2 * lev, LANES))
    for row, mine, diag, thin, n, at_depth in (
            (0, top, dtop, gtop, 0, 0), (clat - 2, bottom, dbottom, gbottom, 1, clat - 1)):
        for q in range(5):
            src = fields.at[HALO_FIELDS[q]] if q < 3 else (frac if q == 3 else helm)
            for k in range(lev):
                mine[q, 2 * k:2 * k + 2, :] = src[k, row:row + 2, :]
        mine[5] = jnp.full((2 * lev, LANES), depth_ref[at_depth].astype(F32))
        copies[2 + n].start()
        u = jnp.where(lane8 < 2, turn(mine[3], 2), mine[0])
        diag[0] = jnp.where(lane8 == 2, turn(mine[4], 3), u)
        diag[1] = mine[1]
        diag[2] = mine[2]
        copies[4 + n].start()
        g = mine[0]
        for q in range(1, 5):
            at = 11 if q == 4 else 3 * q
            g = jnp.where(lane8 >= at, turn(mine[q], at), g)
        thin[...] = g
        copies[6 + n].start()
    for c in copies:
        c.wait()


def interp_weights(frac):
    s = -frac
    below, above = (s - 1.0) * s, (s + 1.0) * (s + 2.0)
    return [
        s * above * (1.0 / 6.0),
        (s - 1.0) * above * -0.5,
        below * (s + 2.0) * 0.5,
        below * (s + 1.0) * (-1.0 / 6.0),
    ]


def depart(own, left, right, depth, weights):
    lane = lane_of(own[0].shape)
    totals = [jnp.zeros_like(own[0]) for _ in own]
    for o, w in zip((-1, 0, 1, 2), weights):
        s = depth + o
        t = lane + s
        shift = (s + LANES) & (LANES - 1)
        for n in range(len(own)):
            x = jnp.where(t <= LANES - 1, own[n], left[n])
            if o == -1:
                x = jnp.where(t == -1, right[n], x)
            totals[n] = totals[n] + w * pltpu.roll(x, shift, axis=1)
    return totals


def depart_beside(own, left, right, depth, weights):
    lane = lane_of(own[0].shape)
    totals = [jnp.zeros_like(own[0]) for _ in own]
    for o, w in zip((-1, 0, 1, 2), weights):
        s = depth + o
        t = lane + s
        shift = (s + LANES) & (LANES - 1)
        for n in range(len(own)):
            x = jnp.where(t <= LANES - 1, left[n], own[n])
            if o < 2:
                x = jnp.where((t >= 0) & (t <= 1), right[n], x)
            if o == -1:
                x = jnp.where(t == -1, own[n], x)
            totals[n] = totals[n] + w * pltpu.roll(x, shift, axis=1)
    return totals


def beside_pair(own, halo):
    lane = lane_of(own.shape)
    first, last = lane == 0, lane == LANES - 1
    return (
        (turn(jnp.where(first, halo, own), -1), turn(jnp.where(last, halo, own), 1)),
        (turn(jnp.where(first, own, halo), -1), turn(jnp.where(last, own, halo), 1)),
    )


def update(lev, clat, *refs):
    sources, (departed_o, pressure_o), (ext, hel, rhs_s, p1_s, wts), here, (departed, pressure), (in_sem, out_sem) = (
        refs[:12], refs[12:14], refs[14:19], refs[19:31], refs[31:33], refs[33:])
    loads = [pltpu.make_async_copy(src, dst, in_sem.at[n]) for n, (src, dst) in enumerate(zip(sources, here))]
    for n in (2, 0, 1, *range(3, len(loads))):
        loads[n].start()
    depth_ref, fields, frac, helm, main, edge, above, below, la, lb, ra, rb = here
    bands = clat // BAND
    loads.pop(2).wait()
    for k in range(lev):
        for o, w in enumerate(interp_weights(frac[k])):
            wts[o, k] = w
    for load in loads:
        load.wait()
    stores = []
    j = lax.axis_index("lat")
    inside = (j > 0, j < lax.axis_size("lat") - 1)
    jet = jet_band(depth_ref, bands)
    nk = lev * BAND
    lane = lane_of((nk, LANES))
    flat = lambda x: x.reshape(nk, LANES)
    deep = lambda x: x.reshape(lev, BAND, LANES)
    pick = lambda z: [z[f] for f in HALO_FIELDS]
    for b in range(bands):
        rows = pl.ds(b * BAND, BAND)
        depth = depth_ref[b * BAND]
        slot = b - (b > jet).astype(jnp.int32)
        amount = (2 * LANES - NEAR - NEAR * slot) & (LANES - 1)
        whole = b == jet
        own = [flat(fields[f, :, rows, :]) for f in range(5)]
        left = [jnp.where(whole, flat(main[0, f]), pltpu.roll(flat(main[1, f]), amount, axis=1)) for f in range(5)]
        brim = flat(edge[...])
        right = [turn(brim, -(32 * b + 3 * f)) for f in range(5)]
        got = depart(own, left, right, depth, [flat(wts[o, :, rows, :]) for o in range(4)])
        rest = flat(main[1, 0])
        fr = jnp.where(lane < 64, turn(brim, -(32 * b + 15)), turn(rest, 18 - 3 * b))
        he = jnp.where(lane < 64, turn(brim, -(32 * b + 17)), turn(rest, 17 - 3 * b))
        past = depart_beside(pick(own), pick(left), pick(right), depth, interp_weights(fr))
        at = pl.ds((b + 1) * BAND, BAND)
        for f in range(5):
            departed[f, :, rows, :] = deep(got[f])
        for q, f in enumerate(HALO_FIELDS):
            ext[q, 0, :, at, :] = deep(got[f])
            ext[q, 1, :, at, :] = deep(past[q])
        hel[0, :, at, :] = helm[:, rows, :]
        hel[1, :, at, :] = deep(he)
        stores.append(pltpu.make_async_copy(departed.at[:, :, rows, :], departed_o.at[:, :, rows, :], out_sem.at[b]))
        stores[-1].start()
    lane = lane_of((BAND, LANES))
    for side, (mine, diag, thin) in enumerate(((above, la, ra), (below, lb, rb))):
        depth = jnp.max(mine[5]).astype(jnp.int32)
        own = [mine[q] for q in range(3)]
        left = [diag[q] for q in range(3)]
        g = thin[...]
        right = [turn(g, -3 * q) for q in range(3)]
        fr = jnp.where(lane < 64, turn(g, -9), turn(left[0], -2))
        he = jnp.where(lane < 64, turn(g, -11), turn(left[0], -3))
        got = depart(own, left, right, depth, interp_weights(mine[3]))
        past = depart_beside(own, left, right, depth, interp_weights(fr))
        at = BAND - 2 if side == 0 else BAND + clat
        for k in range(lev):
            pair = slice(2 * k, 2 * k + 2)
            for q in range(3):
                ext[q, 0, k, at:at + 2, :] = jnp.where(inside[side], got[q], 0.0)[pair]
                ext[q, 1, k, at:at + 2, :] = jnp.where(inside[side], past[q], 0.0)[pair]
            hel[0, k, at:at + 2, :] = mine[4][pair]
            hel[1, k, at:at + 2, :] = he[pair]
    tall = clat + BAND
    row = lax.broadcasted_iota(jnp.int32, (lev, tall, LANES), 1)
    outside = ((row == 0) & jnp.logical_not(inside[0])) | ((row == clat + 1) & jnp.logical_not(inside[1]))
    first = BAND - 1
    flat = lambda x: x.reshape(-1, LANES)
    mid, up, down = pl.ds(first, tall), pl.ds(first - 1, tall), pl.ds(first + 1, tall)
    u_all = beside_pair(flat(ext[0, 0, :, mid, :]), flat(ext[0, 1, :, mid, :]))
    phi = [flat(ext[2, h, :, mid, :]) for h in range(2)]
    phi_all = beside_pair(*phi)
    for h in range(2):
        div = 0.5 * (u_all[h][0] - u_all[h][1] + flat(ext[1, h, :, down, :]) - flat(ext[1, h, :, up, :]))
        rhs = phi[h] - 0.5 * div
        around = phi_all[h][0] + phi_all[h][1] + flat(ext[2, h, :, down, :]) + flat(ext[2, h, :, up, :])
        p1 = (rhs + around) / (4.0 + flat(hel[h, :, mid, :]))
        p1_s[h] = jnp.where(outside, 0.0, p1.reshape(lev, tall, LANES))
        if h == 0:
            rhs_s[...] = rhs.reshape(lev, tall, LANES)
    mid = pl.ds(1, clat)
    east, west = beside_pair(flat(p1_s[0, :, mid, :]), flat(p1_s[1, :, mid, :]))[0]
    around = east + west + flat(p1_s[0, :, pl.ds(2, clat), :]) + flat(p1_s[0, :, pl.ds(0, clat), :])
    pressure[...] = ((flat(rhs_s[:, mid, :]) + around) / (4.0 + flat(helm[...]))).reshape(lev, clat, LANES)
    stores.append(pltpu.make_async_copy(pressure, pressure_o, out_sem.at[bands]))
    stores[-1].start()
    for store in stores:
        store.wait()


def local(fields, depth, frac, helm):
    lev, clat, clon = fields.shape[1:]
    hbm = pl.BlockSpec(memory_space=pltpu.HBM)
    tiles = [(2, 5, lev, BAND, clon), (lev, BAND, clon), (6, 2 * lev, clon), (6, 2 * lev, clon),
             (3, 2 * lev, clon), (3, 2 * lev, clon), (2 * lev, clon), (2 * lev, clon)]
    halos = pl.pallas_call(
        functools.partial(exchange, lev, clat),
        out_shape=[jax.ShapeDtypeStruct(t, F32) for t in tiles],
        in_specs=[hbm] * 4,
        out_specs=[hbm] * len(tiles),
        scratch_shapes=[
            pltpu.SMEM(depth.shape, jnp.int32),
            pltpu.VMEM(fields.shape, F32), pltpu.VMEM(frac.shape, F32), pltpu.VMEM(helm.shape, F32),
            *[pltpu.VMEM(t, F32) for t in tiles],
            pltpu.SemaphoreType.DMA((4,)),
            pltpu.SemaphoreType.DMA((9,)),
            pltpu.SemaphoreType.DMA((9,)),
        ],
        compiler_params=pltpu.CompilerParams(collective_id=0, has_side_effects=True, vmem_limit_bytes=60 << 20),
        name="exchange",
    )(depth, fields, frac, helm)
    tall = clat + 2 * BAND
    return pl.pallas_call(
        functools.partial(update, lev, clat),
        out_shape=[jax.ShapeDtypeStruct(fields.shape, F32), jax.ShapeDtypeStruct(frac.shape, F32)],
        in_specs=[hbm] * (4 + len(tiles)),
        out_specs=[hbm, hbm],
        scratch_shapes=[
            pltpu.VMEM((3, 2, lev, tall, clon), F32),
            pltpu.VMEM((2, lev, tall, clon), F32),
            pltpu.VMEM((lev, clat + BAND, clon), F32),
            pltpu.VMEM((2, lev, clat + BAND, clon), F32),
            pltpu.VMEM((4, *frac.shape), F32),
            pltpu.SMEM(depth.shape, jnp.int32),
            *[pltpu.VMEM(t, F32) for t in (fields.shape, frac.shape, helm.shape, *tiles, fields.shape, frac.shape)],
            pltpu.SemaphoreType.DMA((4 + len(tiles),)),
            pltpu.SemaphoreType.DMA((clat // BAND + 1,)),
        ],
        compiler_params=pltpu.CompilerParams(vmem_limit_bytes=60 << 20),
        name="update",
    )(depth, fields, frac, helm, *halos)


def solution(mesh):
    placed = (P(None, None, "lat", "lon"), P("lat"), P(None, "lat", "lon"), P(None, "lat", "lon"))
    return jax.shard_map(
        local,
        mesh=mesh,
        in_specs=placed,
        out_specs=(P(None, None, "lat", "lon"), P(None, "lat", "lon")),
        check_vma=False,
    )
```
